512 devices in a mesh: ctx: 64 (over z, y_hi, core), head: 8 (over y_lo, x).
Axes of the slice: x: 4, y: 8 (y_hi: 4, y_lo: 2; y = y_hi * 2 + y_lo), z: 8, core: 2. Of those that a mesh axis runs over, the one named last changes fastest.
Arguments:
- query: bfloat16 [8192, 4096], P('ctx', 'head'), may hold values from -11 to 11
- key_proj: bfloat16 [8192, 1024], P(('ctx', 'head')), may hold values from -6 to 6
- value_proj: bfloat16 [8192, 1024], P(('ctx', 'head')), may hold values from -6 to 6
- d_out: bfloat16 [8192, 4096], P('ctx', 'head'), may hold values from -6 to 6
- block_doc: int32 [64], replicated, may hold values from 0 to 2, as said below
- block_mask: int32 [64, 64], replicated, may hold values 0 or 1
Outputs:
- attn_out: bfloat16 [8192, 4096], P('ctx', 'head')
- d_query: bfloat16 [8192, 4096], P('ctx', 'head')
- d_key: bfloat16 [8192, 1024], P(('ctx', 'head'))
- d_value: bfloat16 [8192, 1024], P(('ctx', 'head'))
The draws below stay inside these ranges and needn't reach their ends.
Inputs may be any that keep to these rules, and one draw needn't show every extreme that they name: `block_doc`: ids never fall; each document spans 1 to 35 blocks and one spans exactly 35.
All inputs are finite; a program needn't handle non-finite values.
Results may differ from the reference program's by a relative error of at most 0.04.
Values may be sent and summed in bfloat16 or wider, within the bound.
No kernel may reach another device: no remote copies, remote signals or barrier semaphores. Data moves between devices by JAX's collectives and lax.ppermute only.
A program may use at most 64 MiB of HBM per device.

```python
import jax
import jax.numpy as jnp
from jax import lax

KV_HEADS = 8
HEAD_DIM = 128
Q_PER_KV = 4
BLOCK = 128
TOKENS = 8192
NBLK = 64
DOC_MOST = 35


def draw_key_proj(key, part):
    key = jax.random.fold_in(key, 3)
    drawn = jnp.clip(jax.random.normal(key, (TOKENS, KV_HEADS * HEAD_DIM), jnp.float32), -6.0, 6.0)
    return drawn.astype(jnp.bfloat16)


def draw_query(key, part):
    key = jax.random.fold_in(key, 5)
    width = KV_HEADS * Q_PER_KV * HEAD_DIM
    drawn = jnp.clip(jax.random.normal(key, (TOKENS, width), jnp.float32), -6.0, 6.0)
    return drawn.astype(jnp.bfloat16)


def draw_block_doc(key, part):
    key = jax.random.fold_in(key, 11)
    remain = NBLK - DOC_MOST
    place = jax.random.randint(jax.random.fold_in(key, 1), (), 0, 3, jnp.int32)
    first = jax.random.randint(jax.random.fold_in(key, 2), (), 1, remain, jnp.int32)
    second = remain - first
    length_zero = jnp.where(place == 0, DOC_MOST, first)
    length_one = jnp.where(place == 0, first, jnp.where(place == 1, DOC_MOST, second))
    blocks = jnp.arange(NBLK, dtype=jnp.int32)
    ids = (blocks >= length_zero).astype(jnp.int32) + (blocks >= length_zero + length_one).astype(jnp.int32)
    return ids.astype(jnp.int32)


def plant(result, key, low, high):
    shape = result.shape
    index_at = [jax.random.randint(jax.random.fold_in(key, axis), (), 0, shape[axis]) for axis in range(len(shape))]
    result = result.at[tuple(index_at)].set(low)
    longest = shape.index(max(shape))
    index_at[longest] = (index_at[longest] + 1) % shape[longest]
    return result.at[tuple(index_at)].set(high)


def block_levels(key, extent, split, smallest, high):
    gain, own = 1.0, jax.random.fold_in(key, 6)
    for axis_at, blocks in split:
        steps = jnp.exp(jax.random.uniform(jax.random.fold_in(own, axis_at), (blocks,), jnp.float32, smallest / len(split), high / len(split)))
        gain = gain * jnp.repeat(steps, extent[axis_at] // blocks).reshape([-1 if axis == axis_at else 1 for axis in range(len(extent))])
    return gain


def bell_draw(rng, dims, spread, bound, shards=(), kind=jnp.bfloat16):
    values = spread * jax.random.normal(rng, dims, jnp.float32)
    if shards:
        values = values * block_levels(rng, dims, shards, -0.22, 0.18)
    return jnp.clip(values, -bound, bound).astype(kind)


def setup_inputs(seed: int = 0) -> dict:
    key_list = jax.random.split(jax.random.key(seed), 7)
    return {
        "query": draw_query(jax.random.fold_in(key_list[6], 71), 0),
        "key_proj": draw_key_proj(jax.random.fold_in(key_list[6], 71), 0),
        "value_proj": bell_draw(key_list[2], (TOKENS, KV_HEADS * HEAD_DIM), 1.0, 6.0, ((0, 512),)),
        "d_out": bell_draw(key_list[3], (TOKENS, KV_HEADS * Q_PER_KV * HEAD_DIM), 1.0, 6.0, ((0, 64), (1, 8))),
        "block_doc": draw_block_doc(jax.random.fold_in(key_list[6], 71), 0),
        "block_mask": plant((jax.random.randint(key_list[5], (NBLK, NBLK), 0, 8) < 7).astype(jnp.int32), jax.random.fold_in(key_list[5], 1), 0, 1),
    }


neg_fill = -1e30


def allowed_pairs(q_tok, k_tok, block_doc, block_mask):
    q_blk = q_tok // BLOCK
    k_blk = k_tok // BLOCK
    table = jnp.take(jnp.take(block_mask, q_blk, axis=0), k_blk, axis=1)
    same_doc = jnp.take(block_doc, q_blk)[:, None] == jnp.take(block_doc, k_blk)[None, :]
    earlier = (k_blk[None, :] < q_blk[:, None]) & (table == 1) & same_doc
    diagonal = (k_blk[None, :] == q_blk[:, None]) & (k_tok[None, :] <= q_tok[:, None])
    return earlier | diagonal


def reference(query, key_proj, value_proj, d_out, block_doc, block_mask):
    scale_qk = HEAD_DIM ** -0.5
    key_all = key_proj.astype(jnp.float32).reshape(TOKENS, KV_HEADS, HEAD_DIM)
    value_all = value_proj.astype(jnp.float32).reshape(TOKENS, KV_HEADS, HEAD_DIM)
    all_tok = jnp.arange(TOKENS, dtype=jnp.int32)

    def per_block(carry, blk_id):
        grad_key, grad_value = carry
        start = blk_id * BLOCK
        q_blk = lax.dynamic_slice_in_dim(query, start, BLOCK, 0).astype(jnp.float32)
        q_blk = q_blk.reshape(BLOCK, KV_HEADS, Q_PER_KV, HEAD_DIM)
        do_blk = lax.dynamic_slice_in_dim(d_out, start, BLOCK, 0).astype(jnp.float32)
        do_blk = do_blk.reshape(BLOCK, KV_HEADS, Q_PER_KV, HEAD_DIM)
        q_tok = start + jnp.arange(BLOCK, dtype=jnp.int32)
        allow = allowed_pairs(q_tok, all_tok, block_doc, block_mask)[None, None]
        scores = jnp.einsum('qgjd,kgd->gjqk', q_blk, key_all) * scale_qk
        scores = jnp.where(allow, scores, neg_fill)
        top = jnp.max(scores, axis=-1, keepdims=True)
        expo = jnp.where(allow, jnp.exp(scores - top), 0.0)
        total = jnp.sum(expo, axis=-1, keepdims=True)
        weights16 = lax.optimization_barrier(expo.astype(jnp.bfloat16)).astype(jnp.float32)
        out_blk = (jnp.einsum('gjqk,kgd->gjqd', weights16, value_all) / total).astype(jnp.bfloat16)
        lse = top + jnp.log(total)
        prob = jnp.where(allow, jnp.exp(scores - lse), 0.0)
        do_heads = do_blk.transpose(1, 2, 0, 3)
        delta = jnp.sum(do_heads * out_blk.astype(jnp.float32), axis=-1, keepdims=True)
        d_prob = jnp.einsum('qgjd,kgd->gjqk', do_blk, value_all)
        d_score = prob * (d_prob - delta)
        prob16 = lax.optimization_barrier(prob.astype(jnp.bfloat16)).astype(jnp.float32)
        dscore16 = lax.optimization_barrier(d_score.astype(jnp.bfloat16)).astype(jnp.float32)
        dq_blk = (scale_qk * jnp.einsum('gjqk,kgd->qgjd', dscore16, key_all)).astype(jnp.bfloat16)
        grad_key = grad_key + scale_qk * jnp.einsum('gjqk,qgjd->kgd', dscore16, q_blk)
        grad_value = grad_value + jnp.einsum('gjqk,qgjd->kgd', prob16, do_blk)
        out_rows = out_blk.transpose(2, 0, 1, 3).reshape(BLOCK, KV_HEADS * Q_PER_KV * HEAD_DIM)
        dq_rows = dq_blk.reshape(BLOCK, KV_HEADS * Q_PER_KV * HEAD_DIM)
        return (grad_key, grad_value), (out_rows, dq_rows)

    zeros_kv = jnp.zeros((TOKENS, KV_HEADS, HEAD_DIM), jnp.float32)
    (grad_key, grad_value), (out_rows, dq_rows) = lax.scan(
        per_block, (zeros_kv, zeros_kv), jnp.arange(NBLK, dtype=jnp.int32))
    attn_out = out_rows.reshape(TOKENS, KV_HEADS * Q_PER_KV * HEAD_DIM)
    d_query = dq_rows.reshape(TOKENS, KV_HEADS * Q_PER_KV * HEAD_DIM)
    d_key = grad_key.reshape(TOKENS, KV_HEADS * HEAD_DIM).astype(jnp.bfloat16)
    d_value = grad_value.reshape(TOKENS, KV_HEADS * HEAD_DIM).astype(jnp.bfloat16)
    return (attn_out, d_query, d_key, d_value)
```

```python
import jax
import jax.numpy as jnp
import numpy as np
from jax import lax
from jax.experimental import pallas as pl
from jax.experimental.pallas import tpu as pltpu
from jax.sharding import Mesh
from jax.sharding import PartitionSpec as P

HEAD_DIM = 128
Q_PER_KV = 4
BLOCK = 128
PLANE = 8
ZN = 8
SLOTS = 6
ROWS = Q_PER_KV * BLOCK
SCALE = HEAD_DIM**-0.5
LOG2_SCALE = SCALE * float(np.log2(np.e))
LOW = -1e30
FAR = 2e30

PLANE_AXES = ("y", "c")
HEAD_AXES = ("yl", "x")


def dot_nt(a, b):
    return lax.dot_general(a, b, (((1,), (1,)), ((), ())), preferred_element_type=jnp.float32)


def dot_nn(a, b):
    return lax.dot_general(a, b, (((1,), (0,)), ((), ())), preferred_element_type=jnp.float32)


def rows_of(block):
    return jnp.concatenate([block[:, j * HEAD_DIM : (j + 1) * HEAD_DIM] for j in range(Q_PER_KV)], axis=0)


def penalties(pos, doc, mask, b):
    z, a = pos[0], pos[1]
    q_blk = PLANE * z + b
    oks = []
    for s in range(SLOTS):
        kz = z - (SLOTS - 1) + s
        k_blk = jnp.maximum(PLANE * kz + a, 0)
        seen = (k_blk < q_blk) & (mask[q_blk, k_blk] == 1) & (doc[q_blk] == doc[k_blk])
        oks.append((kz >= 0) & (seen | (k_blk == q_blk)))
    return oks


def key_slot(pos, s):
    return jnp.maximum(pos[0] - (SLOTS - 1) + s, 0)


def diagonal_cut(scores, on_diagonal):
    k_at = lax.broadcasted_iota(jnp.int32, (BLOCK, ROWS), 0)
    q_at = lax.broadcasted_iota(jnp.int32, (BLOCK, ROWS), 1) & (BLOCK - 1)
    return jnp.where((k_at <= q_at) | jnp.logical_not(on_diagonal), scores, LOW)


def stats_kernel(pos, doc, mask, qd_ref, kv_ref, st_ref):
    b = pl.program_id(0)
    oks = penalties(pos, doc, mask, b)
    q = rows_of(qd_ref[0, 0])
    do = rows_of(qd_ref[0, 1])
    scores = []
    top = jnp.full((1, ROWS), LOW, jnp.float32)
    for s in range(SLOTS):
        k = kv_ref[key_slot(pos, s), :, :HEAD_DIM]
        sc = dot_nt(k, q)
        if s == SLOTS - 1:
            sc = diagonal_cut(sc, pos[1] == b)
        scores.append(sc)
        most = jnp.max(sc, axis=0, keepdims=True) * LOG2_SCALE
        top = jnp.maximum(top, jnp.where(oks[s], most, LOW))
    total = jnp.zeros((1, ROWS), jnp.float32)
    inner = jnp.zeros((1, ROWS), jnp.float32)
    for s in range(SLOTS):
        v = kv_ref[key_slot(pos, s), :, HEAD_DIM:]
        w = jnp.exp2(scores[s] * LOG2_SCALE - (top + jnp.where(oks[s], 0.0, FAR)))
        dp = dot_nt(v, do)
        total += jnp.sum(w, axis=0, keepdims=True)
        inner += jnp.sum(w * dp, axis=0, keepdims=True)
    st_ref[0, pl.ds(b, 1), :] = jnp.where(total > 0.0, top + jnp.log2(jnp.maximum(total, 1.0)), LOW)
    st_ref[1, pl.ds(b, 1), :] = inner / jnp.maximum(total, 1.0)


def grads_kernel(pos, doc, mask, st_ref, qd_ref, kv_ref, od_ref, dkv_ref, kt, vt, dk, dv, p16, ds16):
    b = pl.program_id(0)

    @pl.when(b == 0)
    def _():
        dk[...] = jnp.zeros_like(dk)
        dv[...] = jnp.zeros_like(dv)
        for s in range(SLOTS):
            both = kv_ref[key_slot(pos, s)]
            kt[:, s * BLOCK : (s + 1) * BLOCK] = both[:, :HEAD_DIM].T
            vt[:, s * BLOCK : (s + 1) * BLOCK] = both[:, HEAD_DIM:].T

    lse_parts = st_ref[:, 0, pl.ds(b, 1), :]
    delta_parts = st_ref[:, 1, pl.ds(b, 1), :]
    most = jnp.max(lse_parts, axis=0)
    lse = most + jnp.log2(jnp.sum(jnp.exp2(lse_parts - most[None]), axis=0))
    delta = jnp.sum(jnp.exp2(lse_parts - lse[None]) * delta_parts, axis=0)

    oks = penalties(pos, doc, mask, b)
    q = rows_of(qd_ref[0, 0])
    do = rows_of(qd_ref[0, 1])
    for s in range(SLOTS):
        both = kv_ref[key_slot(pos, s)]
        sc = dot_nt(both[:, :HEAD_DIM], q)
        if s == SLOTS - 1:
            sc = diagonal_cut(sc, pos[1] == b)
        p = jnp.exp2(sc * LOG2_SCALE - (lse + jnp.where(oks[s], 0.0, FAR)))
        ds = p * (dot_nt(both[:, HEAD_DIM:], do) - delta)
        p16[s * BLOCK : (s + 1) * BLOCK, :] = p.astype(jnp.bfloat16)
        ds16[s * BLOCK : (s + 1) * BLOCK, :] = ds.astype(jnp.bfloat16)
    dv[...] += dot_nn(p16[...], do)
    dk[...] += dot_nn(ds16[...], q)
    out_t = dot_nn(vt[...], p16[...])
    dq_t = dot_nn(kt[...], ds16[...]) * SCALE
    for j in range(Q_PER_KV):
        lanes = slice(j * HEAD_DIM, (j + 1) * HEAD_DIM)
        od_ref[0, :, lanes] = out_t[:, lanes].T.astype(jnp.bfloat16)
        od_ref[0, :, ROWS + j * HEAD_DIM : ROWS + (j + 1) * HEAD_DIM] = dq_t[:, lanes].T.astype(jnp.bfloat16)

    @pl.when(b == PLANE - 1)
    def _():
        dkv_ref[...] = jnp.zeros_like(dkv_ref)
        for s in range(SLOTS):
            kz = pos[0] - (SLOTS - 1) + s

            @pl.when(kz >= 0)
            def _():
                at = slice(s * BLOCK, (s + 1) * BLOCK)
                where = jnp.maximum(kz, 0)
                dkv_ref[where, :, :HEAD_DIM] = (dk[at, :] * SCALE).astype(jnp.bfloat16)
                dkv_ref[where, :, HEAD_DIM:] = dv[at, :].astype(jnp.bfloat16)


def body(query, key_proj, value_proj, d_out, block_doc, block_mask):
    pos = jnp.stack([lax.axis_index("z"), lax.axis_index(PLANE_AXES)]).astype(jnp.int32)

    def by_head(m):
        return m.reshape(16, 8, HEAD_DIM).transpose(1, 0, 2)

    mine = jnp.concatenate([by_head(key_proj), by_head(value_proj)], axis=2)
    kv = lax.all_to_all(
        jnp.broadcast_to(mine[None], (ZN, 8, 16, 2 * HEAD_DIM)).reshape(ZN * 8, 16, 2 * HEAD_DIM),
        ("z",) + HEAD_AXES,
        0,
        0,
        tiled=True,
    ).reshape(ZN, BLOCK, 2 * HEAD_DIM)
    qd = lax.all_gather(jnp.stack([query, d_out]), PLANE_AXES)

    smem = pl.BlockSpec(memory_space=pltpu.SMEM)
    qd_spec = pl.BlockSpec((1, 2, BLOCK, ROWS), lambda b: (b, 0, 0, 0))
    kv_spec = pl.BlockSpec((ZN, BLOCK, 2 * HEAD_DIM), lambda b: (0, 0, 0))
    params = pltpu.CompilerParams(vmem_limit_bytes=48 * 2**20, dimension_semantics=("arbitrary",))
    stats = pl.pallas_call(
        stats_kernel,
        grid=(PLANE,),
        in_specs=[smem, smem, smem, qd_spec, kv_spec],
        out_specs=pl.BlockSpec((2, PLANE, ROWS), lambda b: (0, 0, 0)),
        out_shape=jax.ShapeDtypeStruct((2, PLANE, ROWS), jnp.float32),
        compiler_params=params,
        name="stats",
    )(pos, block_doc, block_mask, qd, kv)
    stats = lax.all_gather(stats, PLANE_AXES)
    od, dkv = pl.pallas_call(
        grads_kernel,
        grid=(PLANE,),
        in_specs=[
            smem,
            smem,
            smem,
            pl.BlockSpec((PLANE, 2, PLANE, ROWS), lambda b: (0, 0, 0, 0)),
            qd_spec,
            kv_spec,
        ],
        out_specs=[pl.BlockSpec((1, BLOCK, 2 * ROWS), lambda b: (b, 0, 0)), kv_spec],
        out_shape=[
            jax.ShapeDtypeStruct((PLANE, BLOCK, 2 * ROWS), jnp.bfloat16),
            jax.ShapeDtypeStruct((ZN, BLOCK, 2 * HEAD_DIM), jnp.bfloat16),
        ],
        scratch_shapes=[
            pltpu.VMEM((HEAD_DIM, SLOTS * BLOCK), jnp.bfloat16),
            pltpu.VMEM((HEAD_DIM, SLOTS * BLOCK), jnp.bfloat16),
            pltpu.VMEM((SLOTS * BLOCK, HEAD_DIM), jnp.float32),
            pltpu.VMEM((SLOTS * BLOCK, HEAD_DIM), jnp.float32),
            pltpu.VMEM((SLOTS * BLOCK, ROWS), jnp.bfloat16),
            pltpu.VMEM((SLOTS * BLOCK, ROWS), jnp.bfloat16),
        ],
        compiler_params=params,
        name="grads",
    )(pos, block_doc, block_mask, stats, qd, kv)
    od = lax.psum_scatter(od, PLANE_AXES, scatter_dimension=0)
    back = lax.all_to_all(
        dkv.reshape(ZN * 8, 16, 2 * HEAD_DIM), ("z",) + HEAD_AXES, 0, 0, tiled=True
    )
    summed = jnp.sum(back.reshape(ZN, 8, 16, 2 * HEAD_DIM).astype(jnp.float32), axis=0)
    summed = summed.astype(jnp.bfloat16).transpose(1, 0, 2)
    d_key = summed[:, :, :HEAD_DIM].reshape(16, 8 * HEAD_DIM)
    d_value = summed[:, :, HEAD_DIM:].reshape(16, 8 * HEAD_DIM)
    return od[:, :ROWS], od[:, ROWS:], d_key, d_value


def solution(mesh):
    fine = Mesh(mesh.devices.reshape(8, 4, 2, 2, 4), ("z", "y", "c", "yl", "x"))
    ctx, head = ("z", "y", "c"), ("yl", "x")
    wide, narrow = P(ctx, head), P(ctx + head, None)
    return jax.shard_map(
        body,
        mesh=fine,
        in_specs=(wide, narrow, narrow, wide, P(), P()),
        out_specs=(wide, wide, narrow, narrow),
        check_vma=False,
    )
```

```python
import jax
import jax.numpy as jnp
import numpy as np
from jax import lax
from jax.experimental import pallas as pl
from jax.experimental.pallas import tpu as pltpu
from jax.sharding import Mesh
from jax.sharding import PartitionSpec as P

HEAD_DIM = 128
Q_PER_KV = 4
HEADS = 8
BLOCK = 128
PIECE = BLOCK // HEADS
GROUP = 4
YN = 4
ZN = 4
KEYS = ZN * YN
WINDOW = 10
ROWS = Q_PER_KV * BLOCK
NEAR = (WINDOW - 1) * BLOCK
SCALE = HEAD_DIM**-0.5
LOG2_SCALE = SCALE * float(np.log2(np.e))
LOW = -1e30
FAR = 2e30
FAR_BACK = ZN - 1


def dot_nt(a, b):
    return lax.dot_general(a, b, (((1,), (1,)), ((), ())), preferred_element_type=jnp.float32)


def dot_nn(a, b):
    return lax.dot_general(a, b, (((1,), (0,)), ((), ())), preferred_element_type=jnp.float32)


def pack_kernel(q_ref, do_ref, k_ref, v_ref, qd_ref, kv_ref):
    for h in range(HEADS):
        lanes = slice(h * HEAD_DIM, (h + 1) * HEAD_DIM)
        both = jnp.concatenate([k_ref[:, lanes], v_ref[:, lanes]], axis=1)
        for p in range(KEYS):
            kv_ref[h * KEYS + p] = both
    for j in range(Q_PER_KV):
        lanes = slice(j * HEAD_DIM, (j + 1) * HEAD_DIM)
        at = slice(j * BLOCK, (j + 1) * BLOCK)
        qd_ref[0, at, :] = q_ref[:, lanes]
        qd_ref[1, at, :] = do_ref[:, lanes]


def member(pos, j):
    return (pos[1] ^ (j // 2)) * 2 + (pos[3] ^ (j % 2))


def window_of(pos, doc, mask, j):
    zh, zl, y, c = pos[0], pos[1], pos[2], pos[3]
    g = member(pos, j)
    q_blk = 16 * zh + 8 * (g // 2) + 2 * y + g % 2
    ahead = q_blk - (16 * zh + 8 * zl + c)
    last = FAR_BACK * YN + jnp.where(ahead < 0, -1, jnp.minimum(ahead // 2, YN - 1))
    oks = []
    for s in range(WINDOW):
        p = last - (WINDOW - 1) + s
        k_blk = 16 * (zh - FAR_BACK + p // YN) + 8 * zl + 2 * (p % YN) + c
        inside = jnp.maximum(k_blk, 0)
        seen = (inside < q_blk) & (mask[q_blk, inside] == 1) & (doc[q_blk] == doc[inside])
        oks.append((k_blk >= 0) & (seen | (k_blk == q_blk)))
    return pl.multiple_of((last - (WINDOW - 1)) * BLOCK, BLOCK), oks


def owner_of(pos, z):
    return (pos[0] - FAR_BACK + z) & (ZN - 1)


def load_keys(pos, kv_ref, k_scr, v_scr):
    for z in range(ZN):
        owner = owner_of(pos, z)
        for y in range(YN):
            for h in range(HEADS):
                at = (z * YN + y) * BLOCK + h * PIECE
                both = kv_ref[h * KEYS + owner * YN + y]
                k_scr[at : at + PIECE, :] = both[:, :HEAD_DIM]
                v_scr[at : at + PIECE, :] = both[:, HEAD_DIM:]


def diagonal_cut(scores):
    k_at = lax.broadcasted_iota(jnp.int32, (BLOCK, ROWS), 0)
    q_at = lax.broadcasted_iota(jnp.int32, (BLOCK, ROWS), 1) & (BLOCK - 1)
    return jnp.where(k_at <= q_at, scores, LOW)


def stats_kernel(pos, doc, mask, *refs):
    qd_refs, kv_ref = refs[:GROUP], refs[GROUP]
    st_ref, k_scr, v_scr, s_scr, far_scr, row = refs[GROUP + 1 :]
    load_keys(pos, kv_ref, k_scr, v_scr)
    queries = [ref[0] for ref in qd_refs]
    d_outs = [ref[1] for ref in qd_refs]
    windows = [window_of(pos, doc, mask, j) for j in range(GROUP)]
    row[...] = jnp.full((8, ROWS), LOW, jnp.float32)
    for j, (start, oks) in enumerate(windows):

        @pl.when(oks[0])
        def _():
            far = dot_nt(k_scr[pl.ds(start, BLOCK), :], queries[j])
            far_scr[j] = far
            row[j : j + 1, :] = jnp.max(far, axis=0, keepdims=True) * LOG2_SCALE

    tops, totals, inners = [], [], []
    for j, (start, oks) in enumerate(windows):
        near = pl.ds(pl.multiple_of(start + BLOCK, BLOCK), NEAR)
        s_scr[j] = dot_nt(k_scr[near, :], queries[j])
        top = row[j : j + 1, :]
        for s in range(1, WINDOW):
            sc = s_scr[j, (s - 1) * BLOCK : s * BLOCK, :]
            if j == 0 and s == WINDOW - 1:
                sc = diagonal_cut(sc)
                s_scr[j, (s - 1) * BLOCK : s * BLOCK, :] = sc
            most = jnp.max(sc, axis=0, keepdims=True) * LOG2_SCALE
            top = jnp.maximum(top, jnp.where(oks[s], most, LOW))
        dp = dot_nt(v_scr[near, :], d_outs[j])
        total = jnp.zeros((1, ROWS), jnp.float32)
        inner = jnp.zeros((1, ROWS), jnp.float32)
        for s in range(1, WINDOW):
            at = slice((s - 1) * BLOCK, s * BLOCK)
            w = jnp.exp2(s_scr[j, at, :] * LOG2_SCALE - (top + jnp.where(oks[s], 0.0, FAR)))
            total += jnp.sum(w, axis=0, keepdims=True)
            inner += jnp.sum(w * dp[at, :], axis=0, keepdims=True)
        tops.append(top)
        totals.append(total)
        inners.append(inner)
    for j, (start, oks) in enumerate(windows):
        top = tops[j]
        row[0:1, :] = totals[j]
        row[1:2, :] = inners[j]

        @pl.when(oks[0])
        def _():
            w = jnp.exp2(far_scr[j] * LOG2_SCALE - top)
            dp = dot_nt(v_scr[pl.ds(start, BLOCK), :], d_outs[j])
            row[0:1, :] += jnp.sum(w, axis=0, keepdims=True)
            row[1:2, :] += jnp.sum(w * dp, axis=0, keepdims=True)

        total, inner = row[0:1, :], row[1:2, :]
        g = member(pos, j)
        st_ref[pl.ds(g, 1), :] = jnp.where(total > 0.0, top + jnp.log2(jnp.maximum(total, 1.0)), LOW)
        st_ref[pl.ds(GROUP + g, 1), :] = inner / jnp.maximum(total, 1.0)


def row_stats(st_ref, g):
    lse_parts = st_ref[:, pl.ds(g, 1), :]
    delta_parts = st_ref[:, pl.ds(GROUP + g, 1), :]
    most = jnp.max(lse_parts, axis=0)
    lse = most + jnp.log2(jnp.sum(jnp.exp2(lse_parts - most[None]), axis=0))
    delta = jnp.sum(jnp.exp2(lse_parts - lse[None]) * delta_parts, axis=0)
    return lse, delta


def weigh(j, oks, scores, d_probs, lse, delta, p16, ds16):
    for s in range(1, WINDOW):
        at = slice((s - 1) * BLOCK, s * BLOCK)
        sc = scores[at, :]
        if j == 0 and s == WINDOW - 1:
            sc = diagonal_cut(sc)
        p = jnp.exp2(sc * LOG2_SCALE - (lse + jnp.where(oks[s], 0.0, FAR)))
        ds = p * (d_probs[at, :] - delta)
        p16[at, :] = p.astype(jnp.bfloat16)
        ds16[at, :] = ds.astype(jnp.bfloat16)


def weigh_far(scores, d_probs, lse, delta):
    p = jnp.exp2(scores * LOG2_SCALE - lse)
    ds = p * (d_probs - delta)
    return p.astype(jnp.bfloat16), ds.astype(jnp.bfloat16)


def key_grads_kernel(pos, doc, mask, st_ref, *refs):
    qd_refs, kv_ref = refs[:GROUP], refs[GROUP]
    dkv_ref, k_scr, v_scr, dk, dv, p16, ds16 = refs[GROUP + 1 :]
    load_keys(pos, kv_ref, k_scr, v_scr)
    dk[...] = jnp.zeros_like(dk)
    dv[...] = jnp.zeros_like(dv)
    for j in range(GROUP):
        start, oks = window_of(pos, doc, mask, j)
        near = pl.ds(pl.multiple_of(start + BLOCK, BLOCK), NEAR)
        far = pl.ds(start, BLOCK)
        q, do = qd_refs[j][0], qd_refs[j][1]
        lse, delta = row_stats(st_ref, member(pos, j))
        weigh(j, oks, dot_nt(k_scr[near, :], q), dot_nt(v_scr[near, :], do), lse, delta, p16.at[j], ds16.at[j])
        dv[near, :] += dot_nn(p16[j], do)
        dk[near, :] += dot_nn(ds16[j], q)

        @pl.when(oks[0])
        def _():
            p, ds = weigh_far(dot_nt(k_scr[far, :], q), dot_nt(v_scr[far, :], do), lse, delta)
            dv[far, :] += dot_nn(p, do)
            dk[far, :] += dot_nn(ds, q)

    for z in range(ZN):
        owner = owner_of(pos, z)
        for y in range(YN):
            for h in range(HEADS):
                at = (z * YN + y) * BLOCK + h * PIECE
                dkv_ref[h * KEYS + owner * YN + y, :, :HEAD_DIM] = (dk[at : at + PIECE, :] * SCALE).astype(jnp.bfloat16)
                dkv_ref[h * KEYS + owner * YN + y, :, HEAD_DIM:] = dv[at : at + PIECE, :].astype(jnp.bfloat16)


def query_grads_kernel(pos, doc, mask, st_ref, *refs):
    qd_refs, kv_ref = refs[:GROUP], refs[GROUP]
    own_ref, other_ref, k_scr, v_scr, kt, vt, p16, ds16, out_t, dq_t = refs[GROUP + 1 :]
    load_keys(pos, kv_ref, k_scr, v_scr)
    for p in range(KEYS):
        at = slice(p * BLOCK, (p + 1) * BLOCK)
        kt[:, at] = k_scr[at, :].T
        vt[:, at] = v_scr[at, :].T
    for j in range(GROUP):
        start, oks = window_of(pos, doc, mask, j)
        near = pl.ds(pl.multiple_of(start + BLOCK, BLOCK), NEAR)
        far = pl.ds(start, BLOCK)
        q, do = qd_refs[j][0], qd_refs[j][1]
        lse, delta = row_stats(st_ref, member(pos, j))
        weigh(j, oks, dot_nt(k_scr[near, :], q), dot_nt(v_scr[near, :], do), lse, delta, p16.at[j], ds16.at[j])
        out_t[...] = dot_nn(vt[:, near], p16[j])
        dq_t[...] = dot_nn(kt[:, near], ds16[j])

        @pl.when(oks[0])
        def _():
            p, ds = weigh_far(dot_nt(k_scr[far, :], q), dot_nt(v_scr[far, :], do), lse, delta)
            out_t[...] += dot_nn(vt[:, far], p)
            dq_t[...] += dot_nn(kt[:, far], ds)

        to_ref = other_ref if j % 2 else own_ref
        for h in range(Q_PER_KV):
            lanes = slice(h * HEAD_DIM, (h + 1) * HEAD_DIM)
            to_ref[j // 2, :, lanes] = out_t[:, lanes].T.astype(jnp.bfloat16)
            to_ref[j // 2, :, ROWS + h * HEAD_DIM : ROWS + (h + 1) * HEAD_DIM] = (dq_t[:, lanes].T * SCALE).astype(jnp.bfloat16)


def finish_kernel(mine_ref, theirs_ref, back_ref, out_ref, dq_ref, dk_ref, dv_ref):
    total = mine_ref[...].astype(jnp.float32) + theirs_ref[...].astype(jnp.float32)
    out_ref[...] = total[:, :ROWS].astype(jnp.bfloat16)
    dq_ref[...] = total[:, ROWS:].astype(jnp.bfloat16)
    for h in range(HEADS):
        lanes = slice(h * HEAD_DIM, (h + 1) * HEAD_DIM)
        both = sum(back_ref[h * KEYS + p].astype(jnp.float32) for p in range(KEYS))
        dk_ref[:, lanes] = both[:, :HEAD_DIM].astype(jnp.bfloat16)
        dv_ref[:, lanes] = both[:, HEAD_DIM:].astype(jnp.bfloat16)


def bf16(*shape):
    return jax.ShapeDtypeStruct(shape, jnp.bfloat16)


def exchange(block, axis):
    return lax.ppermute(block, axis, [(0, 1), (1, 0)])


def spread(pieces):
    return lax.all_to_all(pieces, ("yl", "x", "zh", "y"), 0, 0, tiled=True)


def call(kernel, operands, smem, out_shape, scratch=(), name=None, limit=40):
    kinds = [pl.BlockSpec(memory_space=pltpu.SMEM if i < smem else pltpu.VMEM) for i in range(len(operands))]
    return pl.pallas_call(
        kernel,
        in_specs=kinds,
        out_shape=out_shape,
        out_specs=jax.tree.map(lambda _: pl.BlockSpec(memory_space=pltpu.VMEM), out_shape),
        scratch_shapes=scratch,
        compiler_params=pltpu.CompilerParams(vmem_limit_bytes=limit * 2**20),
        name=name,
    )(*operands)


def body(query, key_proj, value_proj, d_out, block_doc, block_mask):
    pos = jnp.stack([lax.axis_index(axis) for axis in ("zh", "zl", "y", "c")]).astype(jnp.int32)
    qd, pieces = call(
        pack_kernel,
        (query, d_out, key_proj, value_proj),
        0,
        (bf16(2, ROWS, HEAD_DIM), bf16(HEADS * KEYS, PIECE, 2 * HEAD_DIM)),
        name="pack",
        limit=60,
    )
    kv = spread(pieces)
    above = exchange(qd, "zl")
    held = (qd, exchange(qd, "c"), above, exchange(above, "c"), kv)

    keys_scr = pltpu.VMEM((KEYS * BLOCK, HEAD_DIM), jnp.bfloat16)
    stats = call(
        stats_kernel,
        (pos, block_doc, block_mask, *held),
        3,
        jax.ShapeDtypeStruct((2 * GROUP, ROWS), jnp.float32),
        [
            keys_scr,
            keys_scr,
            pltpu.VMEM((GROUP, NEAR, ROWS), jnp.float32),
            pltpu.VMEM((GROUP, BLOCK, ROWS), jnp.float32),
            pltpu.VMEM((8, ROWS), jnp.float32),
        ],
        name="stats",
    )
    stats = lax.all_gather(stats, ("zl", "c"))
    turned = pltpu.VMEM((HEAD_DIM, KEYS * BLOCK), jnp.bfloat16)
    sums = pltpu.VMEM((KEYS * BLOCK, HEAD_DIM), jnp.float32)
    wide = pltpu.VMEM((GROUP, NEAR, ROWS), jnp.bfloat16)
    flat = pltpu.VMEM((HEAD_DIM, ROWS), jnp.float32)
    operands = (pos, block_doc, block_mask, stats, *held)
    dkv = call(
        key_grads_kernel,
        operands,
        3,
        bf16(HEADS * KEYS, PIECE, 2 * HEAD_DIM),
        [keys_scr, keys_scr, sums, sums, wide, wide],
        name="key_grads",
    )
    back = spread(dkv)
    own, other = call(
        query_grads_kernel,
        operands,
        3,
        (bf16(2, BLOCK, 2 * ROWS), bf16(2, BLOCK, 2 * ROWS)),
        [keys_scr, keys_scr, turned, turned, wide, wide, flat, flat],
        name="query_grads",
    )
    merged = own + exchange(other, "c")
    return call(
        finish_kernel,
        (merged[0], exchange(merged[1], "zl"), back),
        0,
        (bf16(BLOCK, ROWS), bf16(BLOCK, ROWS), bf16(PIECE, HEADS * HEAD_DIM), bf16(PIECE, HEADS * HEAD_DIM)),
        name="finish",
    )


def solution(mesh):
    fine = Mesh(mesh.devices.reshape(4, 2, 4, 2, 2, 4), ("zh", "zl", "y", "c", "yl", "x"))
    ctx, head = ("zh", "zl", "y", "c"), ("yl", "x")
    wide, narrow = P(ctx, head), P(ctx + head, None)
    return jax.shard_map(
        body,
        mesh=fine,
        in_specs=(wide, narrow, narrow, wide, P(), P()),
        out_specs=(wide, wide, narrow, narrow),
        check_vma=False,
    )
```

```python
import jax
import jax.numpy as jnp
import numpy as np
from jax import lax
from jax.experimental import pallas as pl
from jax.experimental.pallas import tpu as pltpu
from jax.sharding import Mesh
from jax.sharding import PartitionSpec as P

HEAD_DIM = 128
Q_PER_KV = 4
HEADS = 8
BLOCK = 128
PIECE = BLOCK // HEADS
GROUP = 4
YN = 4
ZN = 4
KEYS = ZN * YN
WINDOW = 10
ROWS = Q_PER_KV * BLOCK
NEAR = (WINDOW - 1) * BLOCK
SCALE = HEAD_DIM**-0.5
LOG2_SCALE = SCALE * float(np.log2(np.e))
LOW = -1e30
FAR = 2e30
FAR_BACK = ZN - 1


def dot_nt(a, b):
    return lax.dot_general(a, b, (((1,), (1,)), ((), ())), preferred_element_type=jnp.float32)


def dot_nn(a, b):
    return lax.dot_general(a, b, (((1,), (0,)), ((), ())), preferred_element_type=jnp.float32)


def pack_kernel(q_ref, do_ref, k_ref, v_ref, qd_ref, kv_ref):
    for h in range(HEADS):
        lanes = slice(h * HEAD_DIM, (h + 1) * HEAD_DIM)
        both = jnp.concatenate([k_ref[:, lanes], v_ref[:, lanes]], axis=1)
        for p in range(KEYS):
            kv_ref[h * KEYS + p] = both
    for j in range(Q_PER_KV):
        lanes = slice(j * HEAD_DIM, (j + 1) * HEAD_DIM)
        at = slice(j * BLOCK, (j + 1) * BLOCK)
        qd_ref[0, at, :] = q_ref[:, lanes]
        qd_ref[1, at, :] = do_ref[:, lanes]


def member(pos, j):
    return (pos[1] ^ (j // 2)) * 2 + (pos[3] ^ (j % 2))


def window_of(pos, doc, mask, j):
    zh, zl, y, c = pos[0], pos[1], pos[2], pos[3]
    g = member(pos, j)
    q_blk = 16 * zh + 8 * (g // 2) + 2 * y + g % 2
    ahead = q_blk - (16 * zh + 8 * zl + c)
    last = FAR_BACK * YN + jnp.where(ahead < 0, -1, jnp.minimum(ahead // 2, YN - 1))
    oks = []
    for s in range(WINDOW):
        p = last - (WINDOW - 1) + s
        k_blk = 16 * (zh - FAR_BACK + p // YN) + 8 * zl + 2 * (p % YN) + c
        inside = jnp.maximum(k_blk, 0)
        seen = (inside < q_blk) & (mask[q_blk, inside] == 1) & (doc[q_blk] == doc[inside])
        oks.append((k_blk >= 0) & (seen | (k_blk == q_blk)))
    return pl.multiple_of((last - (WINDOW - 1)) * BLOCK, BLOCK), oks


def owner_of(pos, z):
    return (pos[0] - FAR_BACK + z) & (ZN - 1)


def lay_keys(pos, kv_ref, k_ref, v_ref):
    for z in range(ZN):
        owner = owner_of(pos, z)
        for y in range(YN):
            for h in range(HEADS):
                at = (z * YN + y) * BLOCK + h * PIECE
                both = kv_ref[h * KEYS + owner * YN + y]
                k_ref[at : at + PIECE, :] = both[:, :HEAD_DIM]
                v_ref[at : at + PIECE, :] = both[:, HEAD_DIM:]


def diagonal_cut(scores):
    k_at = lax.broadcasted_iota(jnp.int32, (BLOCK, ROWS), 0)
    q_at = lax.broadcasted_iota(jnp.int32, (BLOCK, ROWS), 1) & (BLOCK - 1)
    return jnp.where(k_at <= q_at, scores, LOW)


def first_stats_kernel(pos, doc, mask, qd_a, qd_b, kv_ref, st_ref, k_ref, v_ref, *scratch):
    lay_keys(pos, kv_ref, k_ref, v_ref)
    st_ref[...] = jnp.zeros_like(st_ref)
    stats_of(pos, doc, mask, (0, 1), (qd_a, qd_b), k_ref, v_ref, st_ref, *scratch)


def other_stats_kernel(pos, doc, mask, qd_a, qd_b, k_ref, v_ref, had_ref, st_ref, *scratch):
    st_ref[...] = had_ref[...]
    stats_of(pos, doc, mask, (2, 3), (qd_a, qd_b), k_ref, v_ref, st_ref, *scratch)


def stats_of(pos, doc, mask, members, qd_refs, k_ref, v_ref, st_ref, s_scr, far_scr, row):
    windows = [window_of(pos, doc, mask, j) for j in members]
    row[...] = jnp.full((8, ROWS), LOW, jnp.float32)
    for i, (start, oks) in enumerate(windows):

        @pl.when(oks[0])
        def _():
            far = dot_nt(k_ref[pl.ds(start, BLOCK), :], qd_refs[i][0])
            far_scr[i] = far
            row[i : i + 1, :] = jnp.max(far, axis=0, keepdims=True) * LOG2_SCALE

    nears = [pl.ds(pl.multiple_of(start + BLOCK, BLOCK), NEAR) for start, _ in windows]
    for i, near in enumerate(nears):
        s_scr[i] = dot_nt(k_ref[near, :], qd_refs[i][0])
    d_probs = [dot_nt(v_ref[near, :], qd_refs[i][1]) for i, near in enumerate(nears)]
    tops, totals, inners = [], [], []
    for i, (_, oks) in enumerate(windows):
        top = row[i : i + 1, :]
        for s in range(1, WINDOW):
            sc = s_scr[i, (s - 1) * BLOCK : s * BLOCK, :]
            if members[i] == 0 and s == WINDOW - 1:
                sc = diagonal_cut(sc)
                s_scr[i, (s - 1) * BLOCK : s * BLOCK, :] = sc
            most = jnp.max(sc, axis=0, keepdims=True) * LOG2_SCALE
            top = jnp.maximum(top, jnp.where(oks[s], most, LOW))
        total = jnp.zeros((1, ROWS), jnp.float32)
        inner = jnp.zeros((1, ROWS), jnp.float32)
        for s in range(1, WINDOW):
            at = slice((s - 1) * BLOCK, s * BLOCK)
            w = jnp.exp2(s_scr[i, at, :] * LOG2_SCALE - (top + jnp.where(oks[s], 0.0, FAR)))
            total += jnp.sum(w, axis=0, keepdims=True)
            inner += jnp.sum(w * d_probs[i][at, :], axis=0, keepdims=True)
        tops.append(top)
        totals.append(total)
        inners.append(inner)
    for i, (start, oks) in enumerate(windows):
        top = tops[i]
        row[0:1, :] = totals[i]
        row[1:2, :] = inners[i]

        @pl.when(oks[0])
        def _():
            w = jnp.exp2(far_scr[i] * LOG2_SCALE - top)
            dp = dot_nt(v_ref[pl.ds(start, BLOCK), :], qd_refs[i][1])
            row[0:1, :] += jnp.sum(w, axis=0, keepdims=True)
            row[1:2, :] += jnp.sum(w * dp, axis=0, keepdims=True)

        total, inner = row[0:1, :], row[1:2, :]
        g = member(pos, members[i])
        st_ref[pl.ds(g, 1), :] = jnp.where(total > 0.0, top + jnp.log2(jnp.maximum(total, 1.0)), LOW)
        st_ref[pl.ds(GROUP + g, 1), :] = inner / jnp.maximum(total, 1.0)


def row_stats(st_ref, g):
    lse_parts = st_ref[:, pl.ds(g, 1), :]
    delta_parts = st_ref[:, pl.ds(GROUP + g, 1), :]
    most = jnp.max(lse_parts, axis=0)
    lse = most + jnp.log2(jnp.sum(jnp.exp2(lse_parts - most[None]), axis=0))
    delta = jnp.sum(jnp.exp2(lse_parts - lse[None]) * delta_parts, axis=0)
    return lse, delta


def weigh(j, oks, scores, d_probs, lse, delta, p16, ds16):
    for s in range(1, WINDOW):
        at = slice((s - 1) * BLOCK, s * BLOCK)
        sc = scores[at, :]
        if j == 0 and s == WINDOW - 1:
            sc = diagonal_cut(sc)
        p = jnp.exp2(sc * LOG2_SCALE - (lse + jnp.where(oks[s], 0.0, FAR)))
        ds = p * (d_probs[at, :] - delta)
        p16[at, :] = p.astype(jnp.bfloat16)
        ds16[at, :] = ds.astype(jnp.bfloat16)


def weigh_far(scores, d_probs, lse, delta):
    p = jnp.exp2(scores * LOG2_SCALE - lse)
    ds = p * (d_probs - delta)
    return p.astype(jnp.bfloat16), ds.astype(jnp.bfloat16)


def key_grads_kernel(pos, doc, mask, st_ref, *refs):
    qd_refs = refs[:GROUP]
    k_ref, v_ref, dkv_ref, dk, dv, p16, ds16 = refs[GROUP:]
    dk[...] = jnp.zeros_like(dk)
    dv[...] = jnp.zeros_like(dv)
    windows = [window_of(pos, doc, mask, j) for j in range(GROUP)]
    nears = [pl.ds(pl.multiple_of(start + BLOCK, BLOCK), NEAR) for start, _ in windows]
    rows = [row_stats(st_ref, member(pos, j)) for j in range(GROUP)]

    def products(j):
        return dot_nt(k_ref[nears[j], :], qd_refs[j][0]), dot_nt(v_ref[nears[j], :], qd_refs[j][1])

    ready = products(0)
    for j in range(GROUP):
        now, ready = ready, products(j + 1) if j + 1 < GROUP else None
        weigh(j, windows[j][1], *now, *rows[j], p16.at[j], ds16.at[j])
        dv[nears[j], :] += dot_nn(p16[j], qd_refs[j][1])
        dk[nears[j], :] += dot_nn(ds16[j], qd_refs[j][0])
    for j, (start, oks) in enumerate(windows):
        far = pl.ds(start, BLOCK)

        @pl.when(oks[0])
        def _():
            q, do = qd_refs[j][0], qd_refs[j][1]
            p, ds = weigh_far(dot_nt(k_ref[far, :], q), dot_nt(v_ref[far, :], do), *rows[j])
            dv[far, :] += dot_nn(p, do)
            dk[far, :] += dot_nn(ds, q)

    for z in range(ZN):
        owner = owner_of(pos, z)
        for y in range(YN):
            for h in range(HEADS):
                at = (z * YN + y) * BLOCK + h * PIECE
                dkv_ref[h * KEYS + owner * YN + y, :, :HEAD_DIM] = (dk[at : at + PIECE, :] * SCALE).astype(jnp.bfloat16)
                dkv_ref[h * KEYS + owner * YN + y, :, HEAD_DIM:] = dv[at : at + PIECE, :].astype(jnp.bfloat16)


def query_grads_kernel(pos, doc, mask, st_ref, *refs):
    qd_refs = refs[:GROUP]
    k_scr, v_scr, own_ref, other_ref, kt, vt, p16, ds16, out_t, dq_t = refs[GROUP:]
    for p in range(KEYS):
        at = slice(p * BLOCK, (p + 1) * BLOCK)
        kt[:, at] = k_scr[at, :].T
        vt[:, at] = v_scr[at, :].T
    for j in range(GROUP):
        start, oks = window_of(pos, doc, mask, j)
        near = pl.ds(pl.multiple_of(start + BLOCK, BLOCK), NEAR)
        far = pl.ds(start, BLOCK)
        q, do = qd_refs[j][0], qd_refs[j][1]
        lse, delta = row_stats(st_ref, member(pos, j))
        weigh(j, oks, dot_nt(k_scr[near, :], q), dot_nt(v_scr[near, :], do), lse, delta, p16.at[j], ds16.at[j])
        out_t[...] = dot_nn(vt[:, near], p16[j])
        dq_t[...] = dot_nn(kt[:, near], ds16[j])

        @pl.when(oks[0])
        def _():
            p, ds = weigh_far(dot_nt(k_scr[far, :], q), dot_nt(v_scr[far, :], do), lse, delta)
            out_t[...] += dot_nn(vt[:, far], p)
            dq_t[...] += dot_nn(kt[:, far], ds)

        to_ref = other_ref if j % 2 else own_ref
        for h in range(Q_PER_KV):
            lanes = slice(h * HEAD_DIM, (h + 1) * HEAD_DIM)
            to_ref[j // 2, :, lanes] = out_t[:, lanes].T.astype(jnp.bfloat16)
            to_ref[j // 2, :, ROWS + h * HEAD_DIM : ROWS + (h + 1) * HEAD_DIM] = (dq_t[:, lanes].T * SCALE).astype(jnp.bfloat16)


def finish_kernel(mine_ref, theirs_ref, back_ref, out_ref, dq_ref, dk_ref, dv_ref):
    total = mine_ref[...].astype(jnp.float32) + theirs_ref[...].astype(jnp.float32)
    out_ref[...] = total[:, :ROWS].astype(jnp.bfloat16)
    dq_ref[...] = total[:, ROWS:].astype(jnp.bfloat16)
    for h in range(HEADS):
        lanes = slice(h * HEAD_DIM, (h + 1) * HEAD_DIM)
        both = sum(back_ref[h * KEYS + p].astype(jnp.float32) for p in range(KEYS))
        dk_ref[:, lanes] = both[:, :HEAD_DIM].astype(jnp.bfloat16)
        dv_ref[:, lanes] = both[:, HEAD_DIM:].astype(jnp.bfloat16)


def bf16(*shape):
    return jax.ShapeDtypeStruct(shape, jnp.bfloat16)


def exchange(block, axis):
    return lax.ppermute(block, axis, [(0, 1), (1, 0)])


def spread(pieces):
    return lax.all_to_all(pieces, ("yl", "x", "zh", "y"), 0, 0, tiled=True)


def call(kernel, operands, smem, out_shape, scratch=(), name=None, limit=40):
    kinds = [pl.BlockSpec(memory_space=pltpu.SMEM if i < smem else pltpu.VMEM) for i in range(len(operands))]
    return pl.pallas_call(
        kernel,
        in_specs=kinds,
        out_shape=out_shape,
        out_specs=jax.tree.map(lambda _: pl.BlockSpec(memory_space=pltpu.VMEM), out_shape),
        scratch_shapes=scratch,
        compiler_params=pltpu.CompilerParams(vmem_limit_bytes=limit * 2**20),
        name=name,
    )(*operands)


def body(query, key_proj, value_proj, d_out, block_doc, block_mask):
    pos = jnp.stack([lax.axis_index(axis) for axis in ("zh", "zl", "y", "c")]).astype(jnp.int32)
    qd, pieces = call(
        pack_kernel,
        (query, d_out, key_proj, value_proj),
        0,
        (bf16(2, ROWS, HEAD_DIM), bf16(HEADS * KEYS, PIECE, 2 * HEAD_DIM)),
        name="pack",
        limit=60,
    )
    kv = spread(pieces)
    above = exchange(qd, "zl")
    held = (qd, exchange(qd, "c"), above, exchange(above, "c"))

    keys = bf16(KEYS * BLOCK, HEAD_DIM)
    rows_out = jax.ShapeDtypeStruct((2 * GROUP, ROWS), jnp.float32)
    scratch = [
        pltpu.VMEM((2, NEAR, ROWS), jnp.float32),
        pltpu.VMEM((2, BLOCK, ROWS), jnp.float32),
        pltpu.VMEM((8, ROWS), jnp.float32),
    ]
    places = (pos, block_doc, block_mask)
    stats, k_all, v_all = call(
        first_stats_kernel, (*places, *held[:2], kv), 3, (rows_out, keys, keys), scratch, name="stats_near"
    )
    stats = call(other_stats_kernel, (*places, *held[2:], k_all, v_all, stats), 3, rows_out, scratch, name="stats_above")
    stats = lax.all_gather(stats, ("zl", "c"))
    turned = pltpu.VMEM((HEAD_DIM, KEYS * BLOCK), jnp.bfloat16)
    sums = pltpu.VMEM((KEYS * BLOCK, HEAD_DIM), jnp.float32)
    wide = pltpu.VMEM((GROUP, NEAR, ROWS), jnp.bfloat16)
    flat = pltpu.VMEM((HEAD_DIM, ROWS), jnp.float32)
    operands = (*places, stats, *held, k_all, v_all)
    dkv = call(
        key_grads_kernel,
        operands,
        3,
        bf16(HEADS * KEYS, PIECE, 2 * HEAD_DIM),
        [sums, sums, wide, wide],
        name="key_grads",
    )
    back = spread(dkv)
    own, other = call(
        query_grads_kernel,
        operands,
        3,
        (bf16(2, BLOCK, 2 * ROWS), bf16(2, BLOCK, 2 * ROWS)),
        [turned, turned, wide, wide, flat, flat],
        name="query_grads",
    )
    merged = own + exchange(other, "c")
    return call(
        finish_kernel,
        (merged[0], exchange(merged[1], "zl"), back),
        0,
        (bf16(BLOCK, ROWS), bf16(BLOCK, ROWS), bf16(PIECE, HEADS * HEAD_DIM), bf16(PIECE, HEADS * HEAD_DIM)),
        name="finish",
    )


def solution(mesh):
    fine = Mesh(mesh.devices.reshape(4, 2, 4, 2, 2, 4), ("zh", "zl", "y", "c", "yl", "x"))
    ctx, head = ("zh", "zl", "y", "c"), ("yl", "x")
    wide, narrow = P(ctx, head), P(ctx + head, None)
    return jax.shard_map(
        body,
        mesh=fine,
        in_specs=(wide, narrow, narrow, wide, P(), P()),
        out_specs=(wide, wide, narrow, narrow),
        check_vma=False,
    )
```

```python
import jax
import jax.numpy as jnp
import numpy as np
from jax import lax
from jax.experimental import pallas as pl
from jax.experimental.pallas import tpu as pltpu
from jax.sharding import Mesh
from jax.sharding import PartitionSpec as P

HEAD_DIM = 128
Q_PER_KV = 4
HEADS = 8
BLOCK = 128
PIECE = BLOCK // HEADS
GROUP = 4
YN = 4
ZN = 4
KEYS = ZN * YN
WINDOW = 10
ROWS = Q_PER_KV * BLOCK
NEAR = (WINDOW - 1) * BLOCK
SCALE = HEAD_DIM**-0.5
LOG2_SCALE = SCALE * float(np.log2(np.e))
LOW = -1e30
FAR = 2e30
FAR_BACK = ZN - 1


def dot_nt(a, b):
    return lax.dot_general(a, b, (((1,), (1,)), ((), ())), preferred_element_type=jnp.float32)


def dot_nn(a, b):
    return lax.dot_general(a, b, (((1,), (0,)), ((), ())), preferred_element_type=jnp.float32)


def pack_keys_kernel(k_ref, v_ref, kv_ref):
    for h in range(HEADS):
        lanes = slice(h * HEAD_DIM, (h + 1) * HEAD_DIM)
        both = jnp.concatenate([k_ref[:, lanes], v_ref[:, lanes]], axis=1)
        for p in range(KEYS):
            kv_ref[h * KEYS + p] = both


def pack_queries_kernel(q_ref, do_ref, qd_ref):
    for j in range(Q_PER_KV):
        lanes = slice(j * HEAD_DIM, (j + 1) * HEAD_DIM)
        at = slice(j * BLOCK, (j + 1) * BLOCK)
        qd_ref[0, at, :] = q_ref[:, lanes]
        qd_ref[1, at, :] = do_ref[:, lanes]


def member(pos, j):
    return (pos[1] ^ (j // 2)) * 2 + (pos[3] ^ (j % 2))


def window_of(pos, doc, mask, j):
    zh, zl, y, c = pos[0], pos[1], pos[2], pos[3]
    g = member(pos, j)
    q_blk = 16 * zh + 8 * (g // 2) + 2 * y + g % 2
    ahead = q_blk - (16 * zh + 8 * zl + c)
    last = FAR_BACK * YN + jnp.where(ahead < 0, -1, jnp.minimum(ahead // 2, YN - 1))
    oks = []
    for s in range(WINDOW):
        p = last - (WINDOW - 1) + s
        k_blk = 16 * (zh - FAR_BACK + p // YN) + 8 * zl + 2 * (p % YN) + c
        inside = jnp.maximum(k_blk, 0)
        seen = (inside < q_blk) & (mask[q_blk, inside] == 1) & (doc[q_blk] == doc[inside])
        oks.append((k_blk >= 0) & (seen | (k_blk == q_blk)))
    return pl.multiple_of((last - (WINDOW - 1)) * BLOCK, BLOCK), oks


def owner_of(pos, z):
    return (pos[0] - FAR_BACK + z) & (ZN - 1)


def lay_keys(pos, kv_ref, k_ref, v_ref):
    for z in range(ZN):
        owner = owner_of(pos, z)
        for y in range(YN):
            for h in range(HEADS):
                at = (z * YN + y) * BLOCK + h * PIECE
                both = kv_ref[h * KEYS + owner * YN + y]
                k_ref[at : at + PIECE, :] = both[:, :HEAD_DIM]
                v_ref[at : at + PIECE, :] = both[:, HEAD_DIM:]


def diagonal_cut(scores):
    k_at = lax.broadcasted_iota(jnp.int32, (BLOCK, ROWS), 0)
    q_at = lax.broadcasted_iota(jnp.int32, (BLOCK, ROWS), 1) & (BLOCK - 1)
    return jnp.where(k_at <= q_at, scores, LOW)


def first_stats_kernel(pos, doc, mask, qd_a, qd_b, kv_ref, st_ref, k_ref, v_ref, *scratch):
    lay_keys(pos, kv_ref, k_ref, v_ref)
    st_ref[...] = jnp.zeros_like(st_ref)
    stats_of(pos, doc, mask, (0, 1), (qd_a, qd_b), k_ref, v_ref, st_ref, *scratch)


def other_stats_kernel(pos, doc, mask, qd_a, qd_b, k_ref, v_ref, had_ref, st_ref, *scratch):
    st_ref[...] = had_ref[...]
    stats_of(pos, doc, mask, (2, 3), (qd_a, qd_b), k_ref, v_ref, st_ref, *scratch)


def stats_of(pos, doc, mask, members, qd_refs, k_ref, v_ref, st_ref, s_scr, far_scr, row):
    windows = [window_of(pos, doc, mask, j) for j in members]
    row[...] = jnp.full((8, ROWS), LOW, jnp.float32)
    for i, (start, oks) in enumerate(windows):

        @pl.when(oks[0])
        def _():
            far = dot_nt(k_ref[pl.ds(start, BLOCK), :], qd_refs[i][0])
            far_scr[i] = far
            row[i : i + 1, :] = jnp.max(far, axis=0, keepdims=True) * LOG2_SCALE

    nears = [pl.ds(pl.multiple_of(start + BLOCK, BLOCK), NEAR) for start, _ in windows]
    for i, near in enumerate(nears):
        s_scr[i] = dot_nt(k_ref[near, :], qd_refs[i][0])
    d_probs = [dot_nt(v_ref[near, :], qd_refs[i][1]) for i, near in enumerate(nears)]
    tops, totals, inners = [], [], []
    for i, (_, oks) in enumerate(windows):
        top = row[i : i + 1, :]
        for s in range(1, WINDOW):
            sc = s_scr[i, (s - 1) * BLOCK : s * BLOCK, :]
            if members[i] == 0 and s == WINDOW - 1:
                sc = diagonal_cut(sc)
                s_scr[i, (s - 1) * BLOCK : s * BLOCK, :] = sc
            most = jnp.max(sc, axis=0, keepdims=True) * LOG2_SCALE
            top = jnp.maximum(top, jnp.where(oks[s], most, LOW))
        total = jnp.zeros((1, ROWS), jnp.float32)
        inner = jnp.zeros((1, ROWS), jnp.float32)
        for s in range(1, WINDOW):
            at = slice((s - 1) * BLOCK, s * BLOCK)
            w = jnp.exp2(s_scr[i, at, :] * LOG2_SCALE - (top + jnp.where(oks[s], 0.0, FAR)))
            total += jnp.sum(w, axis=0, keepdims=True)
            inner += jnp.sum(w * d_probs[i][at, :], axis=0, keepdims=True)
        tops.append(top)
        totals.append(total)
        inners.append(inner)
    for i, (start, oks) in enumerate(windows):
        top = tops[i]
        row[0:1, :] = totals[i]
        row[1:2, :] = inners[i]

        @pl.when(oks[0])
        def _():
            w = jnp.exp2(far_scr[i] * LOG2_SCALE - top)
            dp = dot_nt(v_ref[pl.ds(start, BLOCK), :], qd_refs[i][1])
            row[0:1, :] += jnp.sum(w, axis=0, keepdims=True)
            row[1:2, :] += jnp.sum(w * dp, axis=0, keepdims=True)

        total, inner = row[0:1, :], row[1:2, :]
        g = member(pos, members[i])
        st_ref[pl.ds(g, 1), :] = jnp.where(total > 0.0, top + jnp.log2(jnp.maximum(total, 1.0)), LOW)
        st_ref[pl.ds(GROUP + g, 1), :] = inner / jnp.maximum(total, 1.0)


def row_stats(st_ref, g):
    lse_parts = st_ref[:, pl.ds(g, 1), :]
    delta_parts = st_ref[:, pl.ds(GROUP + g, 1), :]
    most = jnp.max(lse_parts, axis=0)
    lse = most + jnp.log2(jnp.sum(jnp.exp2(lse_parts - most[None]), axis=0))
    delta = jnp.sum(jnp.exp2(lse_parts - lse[None]) * delta_parts, axis=0)
    return lse, delta


def weigh(j, oks, scores, d_probs, lse, delta, p16, ds16):
    for s in range(1, WINDOW):
        at = slice((s - 1) * BLOCK, s * BLOCK)
        sc = scores[at, :]
        if j == 0 and s == WINDOW - 1:
            sc = diagonal_cut(sc)
        p = jnp.exp2(sc * LOG2_SCALE - (lse + jnp.where(oks[s], 0.0, FAR)))
        ds = p * (d_probs[at, :] - delta)
        p16[at, :] = p.astype(jnp.bfloat16)
        ds16[at, :] = ds.astype(jnp.bfloat16)


def weigh_far(scores, d_probs, lse, delta):
    p = jnp.exp2(scores * LOG2_SCALE - lse)
    ds = p * (d_probs - delta)
    return p.astype(jnp.bfloat16), ds.astype(jnp.bfloat16)


def key_grads_kernel(pos, doc, mask, st_ref, *refs):
    qd_refs = refs[:GROUP]
    k_ref, v_ref, dkv_ref, dk, dv, p16, ds16 = refs[GROUP:]
    dk[...] = jnp.zeros_like(dk)
    dv[...] = jnp.zeros_like(dv)
    windows = [window_of(pos, doc, mask, j) for j in range(GROUP)]
    nears = [pl.ds(pl.multiple_of(start + BLOCK, BLOCK), NEAR) for start, _ in windows]
    rows = [row_stats(st_ref, member(pos, j)) for j in range(GROUP)]

    def products(j):
        return dot_nt(k_ref[nears[j], :], qd_refs[j][0]), dot_nt(v_ref[nears[j], :], qd_refs[j][1])

    ready = products(0)
    for j in range(GROUP):
        now, ready = ready, products(j + 1) if j + 1 < GROUP else None
        weigh(j, windows[j][1], *now, *rows[j], p16.at[j], ds16.at[j])
        dv[nears[j], :] += dot_nn(p16[j], qd_refs[j][1])
        dk[nears[j], :] += dot_nn(ds16[j], qd_refs[j][0])
    for j, (start, oks) in enumerate(windows):
        far = pl.ds(start, BLOCK)

        @pl.when(oks[0])
        def _():
            q, do = qd_refs[j][0], qd_refs[j][1]
            p, ds = weigh_far(dot_nt(k_ref[far, :], q), dot_nt(v_ref[far, :], do), *rows[j])
            dv[far, :] += dot_nn(p, do)
            dk[far, :] += dot_nn(ds, q)

    for z in range(ZN):
        owner = owner_of(pos, z)
        for y in range(YN):
            for h in range(HEADS):
                at = (z * YN + y) * BLOCK + h * PIECE
                dkv_ref[h * KEYS + owner * YN + y, :, :HEAD_DIM] = (dk[at : at + PIECE, :] * SCALE).astype(jnp.bfloat16)
                dkv_ref[h * KEYS + owner * YN + y, :, HEAD_DIM:] = dv[at : at + PIECE, :].astype(jnp.bfloat16)


def query_grads_kernel(pos, doc, mask, st_ref, *refs):
    qd_refs = refs[:GROUP]
    k_scr, v_scr, own_ref, other_ref, kt, vt, p16, ds16, out_t, dq_t = refs[GROUP:]
    for p in range(KEYS):
        at = slice(p * BLOCK, (p + 1) * BLOCK)
        kt[:, at] = k_scr[at, :].T
        vt[:, at] = v_scr[at, :].T
    for j in range(GROUP):
        start, oks = window_of(pos, doc, mask, j)
        near = pl.ds(pl.multiple_of(start + BLOCK, BLOCK), NEAR)
        far = pl.ds(start, BLOCK)
        q, do = qd_refs[j][0], qd_refs[j][1]
        lse, delta = row_stats(st_ref, member(pos, j))
        weigh(j, oks, dot_nt(k_scr[near, :], q), dot_nt(v_scr[near, :], do), lse, delta, p16.at[j], ds16.at[j])
        out_t[...] = dot_nn(vt[:, near], p16[j])
        dq_t[...] = dot_nn(kt[:, near], ds16[j])

        @pl.when(oks[0])
        def _():
            p, ds = weigh_far(dot_nt(k_scr[far, :], q), dot_nt(v_scr[far, :], do), lse, delta)
            out_t[...] += dot_nn(vt[:, far], p)
            dq_t[...] += dot_nn(kt[:, far], ds)

        to_ref = other_ref if j % 2 else own_ref
        for h in range(Q_PER_KV):
            lanes = slice(h * HEAD_DIM, (h + 1) * HEAD_DIM)
            to_ref[j // 2, :, lanes] = out_t[:, lanes].T.astype(jnp.bfloat16)
            to_ref[j // 2, :, ROWS + h * HEAD_DIM : ROWS + (h + 1) * HEAD_DIM] = (dq_t[:, lanes].T * SCALE).astype(jnp.bfloat16)


def finish_kernel(mine_ref, theirs_ref, back_ref, out_ref, dq_ref, dk_ref, dv_ref):
    total = mine_ref[...].astype(jnp.float32) + theirs_ref[...].astype(jnp.float32)
    out_ref[...] = total[:, :ROWS].astype(jnp.bfloat16)
    dq_ref[...] = total[:, ROWS:].astype(jnp.bfloat16)
    for h in range(HEADS):
        lanes = slice(h * HEAD_DIM, (h + 1) * HEAD_DIM)
        both = sum(back_ref[h * KEYS + p].astype(jnp.float32) for p in range(KEYS))
        dk_ref[:, lanes] = both[:, :HEAD_DIM].astype(jnp.bfloat16)
        dv_ref[:, lanes] = both[:, HEAD_DIM:].astype(jnp.bfloat16)


def bf16(*shape):
    return jax.ShapeDtypeStruct(shape, jnp.bfloat16)


def exchange(block, axis):
    return lax.ppermute(block, axis, [(0, 1), (1, 0)])


def spread(pieces):
    return lax.all_to_all(pieces, ("yl", "x", "zh", "y"), 0, 0, tiled=True)


def call(kernel, operands, smem, out_shape, scratch=(), name=None, limit=40):
    kinds = [pl.BlockSpec(memory_space=pltpu.SMEM if i < smem else pltpu.VMEM) for i in range(len(operands))]
    return pl.pallas_call(
        kernel,
        in_specs=kinds,
        out_shape=out_shape,
        out_specs=jax.tree.map(lambda _: pl.BlockSpec(memory_space=pltpu.VMEM), out_shape),
        scratch_shapes=scratch,
        compiler_params=pltpu.CompilerParams(vmem_limit_bytes=limit * 2**20),
        name=name,
    )(*operands)


def body(query, key_proj, value_proj, d_out, block_doc, block_mask):
    pos = jnp.stack([lax.axis_index(axis) for axis in ("zh", "zl", "y", "c")]).astype(jnp.int32)
    pieces = call(
        pack_keys_kernel,
        (key_proj, value_proj),
        0,
        bf16(HEADS * KEYS, PIECE, 2 * HEAD_DIM),
        name="pack_keys",
        limit=60,
    )
    qd = call(pack_queries_kernel, (query, d_out), 0, bf16(2, ROWS, HEAD_DIM), name="pack_queries")
    kv = spread(pieces)
    above = exchange(qd, "zl")
    held = (qd, exchange(qd, "c"))

    keys = bf16(KEYS * BLOCK, HEAD_DIM)
    rows_out = jax.ShapeDtypeStruct((2 * GROUP, ROWS), jnp.float32)
    scratch = [
        pltpu.VMEM((2, NEAR, ROWS), jnp.float32),
        pltpu.VMEM((2, BLOCK, ROWS), jnp.float32),
        pltpu.VMEM((8, ROWS), jnp.float32),
    ]
    places = (pos, block_doc, block_mask)
    stats, k_all, v_all = call(
        first_stats_kernel, (*places, *held[:2], kv), 3, (rows_out, keys, keys), scratch, name="stats_near"
    )
    above, stats, k_all, v_all = lax.optimization_barrier((above, stats, k_all, v_all))
    held += (above, exchange(above, "c"))
    stats = call(other_stats_kernel, (*places, *held[2:], k_all, v_all, stats), 3, rows_out, scratch, name="stats_above")
    stats = lax.all_gather(stats, ("zl", "c"))
    turned = pltpu.VMEM((HEAD_DIM, KEYS * BLOCK), jnp.bfloat16)
    sums = pltpu.VMEM((KEYS * BLOCK, HEAD_DIM), jnp.float32)
    wide = pltpu.VMEM((GROUP, NEAR, ROWS), jnp.bfloat16)
    flat = pltpu.VMEM((HEAD_DIM, ROWS), jnp.float32)
    operands = (*places, stats, *held, k_all, v_all)
    dkv = call(
        key_grads_kernel,
        operands,
        3,
        bf16(HEADS * KEYS, PIECE, 2 * HEAD_DIM),
        [sums, sums, wide, wide],
        name="key_grads",
    )
    back = spread(dkv)
    own, other = call(
        query_grads_kernel,
        operands,
        3,
        (bf16(2, BLOCK, 2 * ROWS), bf16(2, BLOCK, 2 * ROWS)),
        [turned, turned, wide, wide, flat, flat],
        name="query_grads",
    )
    merged = own + exchange(other, "c")
    return call(
        finish_kernel,
        (merged[0], exchange(merged[1], "zl"), back),
        0,
        (bf16(BLOCK, ROWS), bf16(BLOCK, ROWS), bf16(PIECE, HEADS * HEAD_DIM), bf16(PIECE, HEADS * HEAD_DIM)),
        name="finish",
    )


def solution(mesh):
    fine = Mesh(mesh.devices.reshape(4, 2, 4, 2, 2, 4), ("zh", "zl", "y", "c", "yl", "x"))
    ctx, head = ("zh", "zl", "y", "c"), ("yl", "x")
    wide, narrow = P(ctx, head), P(ctx + head, None)
    return jax.shard_map(
        body,
        mesh=fine,
        in_specs=(wide, narrow, narrow, wide, P(), P()),
        out_specs=(wide, wide, narrow, narrow),
        check_vma=False,
    )
```
